32 devices in a mesh: groups: 2 (over y), ctx: 8 (over z, x), pb: 2 (over core).
Axes of the slice: x: 2, y: 2, z: 4, core: 2. Of those that a mesh axis runs over, the one named last changes fastest.
Arguments:
- att_query: bfloat16 [4, 8, 36864], P(('groups', 'pb'), 'ctx'), parts along dimension 0, may hold values from -26 to 26
- latent_cache: bfloat16 [4096, 576], P(('groups', 'ctx')), parts along dimension 0, may hold values from -6 to 6
- index_query: bfloat16 [4, 8, 4096], P(('groups', 'pb')), parts along dimension 0, may hold values from -70 to 70
- index_weight: float32 [4, 8, 32], P(('groups', 'pb')), parts along dimension 0, may hold values from -4 to 4
- index_keys: bfloat16 [4096, 128], P(('groups', 'ctx')), parts along dimension 0, may hold values from -16 to 16
- selected: int32 [4, 8, 1024], P(('groups', 'pb'), 'ctx'), parts along dimension 0, may hold values from 0 to 2047, as said below
Outputs:
- attended: bfloat16 [4, 8, 32768], P(('groups', 'pb'), 'ctx'), parts along dimension 0
- log_share: float32 [4, 8], P(('groups', 'pb')), parts along dimension 0
The draws below stay inside these ranges and needn't reach their ends.
There are 2 independent parts, one for each index of `groups`. The reference program is written for one: setup_inputs(seed, part) draws one part's arguments, and reference() takes and returns one part's arrays. A program takes and returns all parts, laid end to end along the dimension named above; each array names one. Nothing has to cross between parts.
Inputs may be any that keep to these rules, and one draw needn't show every extreme that they name: `selected`: each query's 1024 positions are distinct, ascending, no later than its own position, and include its own position and the one before. In each query's list at most 256 positions fall in any aligned block of 256 keys, and in every draw some such block holds exactly 256 positions of every query.
All inputs are finite; a program needn't handle non-finite values.
Results may differ from the reference program's by a relative error of at most 0.01.
Values may be sent and summed in bfloat16 or wider, within the bound.
No kernel may reach another device: no remote copies, remote signals or barrier semaphores. Data moves between devices by JAX's collectives and lax.ppermute only.
A program may use at most 64 MiB of HBM per device.

```python
import math
import jax
import jax.numpy as jnp
from jax import lax

HEADS = 64
LATENT = 512
ROPE = 64
IHEADS = 32
IWIDTH = 128
TOPK = 1024
KEY_DEV = 256
KEYS = 2048
QB = 8
QBLOCKS = 2
QUERIES = 16
CAP = 256


def index_weights(key):
    return jnp.clip(jax.random.normal(jax.random.fold_in(key, 3), (QUERIES, IHEADS), jnp.float32), -4.0, 4.0)


def draw_latent_cache(key, part):
    values = jnp.clip(jax.random.normal(jax.random.fold_in(key, 1), (KEYS, LATENT + ROPE), jnp.float32), -6.0, 6.0)
    return values.astype(jnp.bfloat16)


def draw_att_query(key, part):
    values = jnp.clip(jax.random.normal(jax.random.fold_in(key, 2), (QUERIES, HEADS, LATENT + ROPE), jnp.float32), -6.0, 6.0) * 1.5
    return values.reshape(QBLOCKS, QB, HEADS * (LATENT + ROPE)).astype(jnp.bfloat16)


def draw_index_weight(key, part):
    return index_weights(key).reshape(QBLOCKS, QB, IHEADS)


def draw_index_query(key, part):
    values = jnp.clip(jax.random.normal(jax.random.fold_in(key, 4), (QUERIES, IHEADS, IWIDTH), jnp.float32), -4.0, 4.0)
    spread = jnp.exp(jax.random.uniform(jax.random.fold_in(key, 5), (QUERIES, 1, 1), jnp.float32, math.log(0.6), math.log(6.0)))
    values = values * spread
    return values.reshape(QBLOCKS, QB, IHEADS * IWIDTH).astype(jnp.bfloat16)


def draw_index_keys(key, part):
    values = jnp.clip(jax.random.normal(jax.random.fold_in(key, 6), (KEYS, IWIDTH), jnp.float32), -4.0, 4.0)
    spread = jnp.exp(jax.random.uniform(jax.random.fold_in(key, 7), (KEYS, 1), jnp.float32, math.log(0.4), math.log(4.0)))
    values = values * spread
    return values.astype(jnp.bfloat16)


def draw_selected(key, part):
    shards = KEYS // KEY_DEV
    capacity = CAP
    full_key, multiple_key, picking_key = jax.random.split(jax.random.fold_in(key, 11), 3)
    full_shard = jax.random.randint(full_key, (), 0, shards - 1)
    multiples = jax.random.randint(multiple_key, (QUERIES, shards), 1, 5)
    query_keys = jax.random.split(picking_key, QUERIES)
    positions = KEYS - QUERIES + jnp.arange(QUERIES)
    shard_ids = jnp.arange(shards)
    starts = shard_ids * KEY_DEV
    offsets_in = jnp.arange(KEY_DEV)
    global_places = starts[:, None] + offsets_in[None, :]

    def one_query(position, multiple, query_key):
        available = jnp.clip(position - starts + 1, 0, KEY_DEV)
        required = (shard_ids == position // KEY_DEV).astype(jnp.int32) + (shard_ids == (position - 1) // KEY_DEV).astype(jnp.int32)
        is_full = shard_ids == full_shard
        room = jnp.where(is_full, 0, jnp.minimum(capacity, available) - required)
        weight = jnp.where(is_full, 0, (shard_ids + 1) * multiple)
        remaining = TOPK - capacity - jnp.sum(jnp.where(is_full, 0, required))
        portion = jnp.minimum(room, remaining * weight // jnp.sum(weight))
        leftover = remaining - jnp.sum(portion)
        spare_room = (room - portion)[::-1]
        before = jnp.cumsum(spare_room) - spare_room
        topping = jnp.clip(leftover - before, 0, spare_room)[::-1]
        counts = jnp.where(is_full, capacity, required + portion + topping)
        orders = jax.vmap(lambda shard_key: jax.random.permutation(shard_key, KEY_DEV))(jax.random.split(query_key, shards))
        ranking = jnp.where(global_places == position, -2, jnp.where(global_places == position - 1, -1, jnp.where(global_places <= position, orders, KEY_DEV + offsets_in[None, :])))
        rank_of = jnp.argsort(jnp.argsort(ranking, axis=1, stable=True), axis=1, stable=True)
        chosen = rank_of < counts[:, None]
        order_score = jnp.where(chosen, KEYS - global_places, -1 - global_places).reshape(-1)
        values, unused = lax.top_k(order_score, TOPK)
        return (KEYS - values).astype(jnp.int32)
    selections = jax.vmap(one_query)(positions, multiples, query_keys)
    return selections.reshape(QBLOCKS, QB, TOPK)


def setup_inputs(seed: int = 0, part: int = 0) -> dict:
    arg_keys = jax.random.split(jax.random.key(seed), 7)
    part_splits = jax.random.split(jax.random.fold_in(arg_keys[6], part), 7)
    return {
        "att_query": draw_att_query(jax.random.fold_in(jax.random.fold_in(arg_keys[6], part), 71), part),
        "latent_cache": draw_latent_cache(jax.random.fold_in(jax.random.fold_in(arg_keys[6], part), 71), part),
        "index_query": draw_index_query(jax.random.fold_in(jax.random.fold_in(arg_keys[6], part), 71), part),
        "index_weight": draw_index_weight(jax.random.fold_in(jax.random.fold_in(arg_keys[6], part), 71), part),
        "index_keys": draw_index_keys(jax.random.fold_in(jax.random.fold_in(arg_keys[6], part), 71), part),
        "selected": draw_selected(jax.random.fold_in(jax.random.fold_in(arg_keys[6], part), 71), part),
    }


score_scale = 192.0 ** -0.5
floor_value = -1.0e30


def attend_query(latent_cache, query_rows, chosen):
    key_rows = jnp.take(latent_cache, chosen, axis=0).astype(jnp.float32)
    scores = jnp.einsum("hd,kd->hk", query_rows.astype(jnp.float32), key_rows) * score_scale
    highest = jnp.max(scores, axis=1, keepdims=True)
    expo = jnp.exp(scores - highest)
    total = jnp.sum(expo, axis=1, keepdims=True)
    rounded = lax.optimization_barrier(expo.astype(jnp.bfloat16))
    weights = rounded.astype(jnp.float32)
    mixed = jnp.einsum("hk,kd->hd", weights, key_rows[:, :LATENT])
    return (mixed / total).astype(jnp.bfloat16)


def masked_lse(scores, keep_mask):
    highest = jnp.max(jnp.where(keep_mask, scores, floor_value), axis=1)
    summed = jnp.sum(jnp.where(keep_mask, jnp.exp(scores - highest[:, None]), 0.0), axis=1)
    return highest + jnp.log(summed)


def index_block(query_rows, weight_rows, chosen, positions, index_keys):
    row_count = query_rows.shape[0]
    stacked = query_rows.reshape(row_count * IHEADS, IWIDTH)
    products = jnp.dot(stacked, index_keys.T, preferred_element_type=jnp.float32)
    rectified = jnp.maximum(products, 0.0).reshape(row_count, IHEADS, KEYS)
    index_scale = float(IHEADS * IWIDTH) ** -0.5
    scores = jnp.sum(weight_rows[:, :, None] * rectified, axis=1) * index_scale
    key_places = jnp.arange(KEYS).astype(jnp.int32)
    causal = key_places[None, :] <= positions[:, None]
    all_lse = masked_lse(scores, causal)
    picked = jnp.take_along_axis(scores, chosen, axis=1)
    sel_highest = jnp.max(picked, axis=1)
    sel_lse = sel_highest + jnp.log(jnp.sum(jnp.exp(picked - sel_highest[:, None]), axis=1))
    return sel_lse - all_lse


def reference(att_query, latent_cache, index_query, index_weight, index_keys, selected):
    selections = selected.reshape(QUERIES, TOPK)
    queries = att_query.reshape(QUERIES, HEADS, LATENT + ROPE)
    attended = lax.map(lambda paired: attend_query(latent_cache, paired[0], paired[1]), (queries, selections))
    positions = (KEYS - QUERIES + jnp.arange(QUERIES)).astype(jnp.int32)
    groups_count = QUERIES // 8
    shares = lax.map(
        lambda grouped: index_block(grouped[0], grouped[1], grouped[2], grouped[3], index_keys),
        (index_query.reshape(groups_count, 8, IHEADS * IWIDTH),
         index_weight.reshape(groups_count, 8, IHEADS),
         selections.reshape(groups_count, 8, TOPK),
         positions.reshape(groups_count, 8)))
    return attended.reshape(QBLOCKS, QB, HEADS * LATENT), shares.reshape(QBLOCKS, QB)
```

```python
import functools

import jax
import jax.numpy as jnp
from jax import lax
from jax.experimental import pallas as pl
from jax.experimental.pallas import tpu as pltpu
from jax.sharding import PartitionSpec as P

HEADS = 64
LATENT = 512
LANES = 128
SPAN = 4

score_scale = 192.0 ** (-0.5)
floor_value = -1e30

NT = (((1,), (1,)), ((), ()))
NN = (((1,), (0,)), ((), ()))


def round_up(count, step):
    return -(-count // step) * step


def swap(x, offset):
    size = lax.axis_size("ctx")
    return lax.ppermute(x, "ctx", [(i, i ^ offset) for i in range(size)])


def swap_cores(x):
    size = lax.axis_size("pb")
    return lax.ppermute(x, "pb", [(i, i ^ 1) for i in range(size)])


def swap_apart(x, even_offset, odd_offset):
    size, cores = lax.axis_size("ctx"), lax.axis_size("pb")
    moves = []
    for i in range(size):
        for c in range(cores):
            partner = i ^ (odd_offset if c % 2 else even_offset)
            moves.append((i * cores + c, partner * cores + c))
    return lax.ppermute(x, ("ctx", "pb"), moves)


def call(kernel, out_shape, scratch=(), **kwargs):
    return pl.pallas_call(
        kernel,
        out_shape=out_shape,
        scratch_shapes=list(scratch),
        compiler_params=pltpu.CompilerParams(vmem_limit_bytes=40 * 2**20),
        **kwargs,
    )


def prepare_kernel(query_ref, index_query_ref, weight_ref, keys_ref, list_ref, packed_ref, share_ref):
    keys_here, width = keys_ref.shape
    rows, head_count = weight_ref.shape
    shards = share_ref.shape[0] - rows
    top_count = list_ref.shape[1]
    row_width = query_ref.shape[1]
    places = list_ref[...]
    low = places % LANES
    high = places // LANES
    low_hot = (lax.broadcasted_iota(jnp.int32, (LANES, top_count), 0) == low).astype(jnp.bfloat16)
    part_count = keys_here // LANES
    owner = lax.broadcasted_iota(jnp.int32, (shards, top_count), 0) * part_count
    parts = []
    for part in range(part_count):
        high_hot = (owner + part == high).astype(jnp.bfloat16)
        parts.append(lax.dot_general(high_hot, low_hot, NT, preferred_element_type=jnp.float32))
    mask = jnp.concatenate(parts, axis=1)
    pad_rows = packed_ref.shape[0] - HEADS - shards
    wide = jnp.concatenate([mask, jnp.zeros((shards, row_width - keys_here), jnp.float32)], axis=1)
    if pad_rows:
        wide = jnp.concatenate([wide, jnp.zeros((pad_rows, row_width), jnp.float32)], axis=0)
    packed_ref[HEADS:, :] = wide.astype(jnp.bfloat16)
    packed_ref[:HEADS, :] = query_ref[...]
    stacked = jnp.concatenate(
        [index_query_ref[:, h * width : (h + 1) * width].astype(jnp.float32) for h in range(head_count)], axis=0
    ).astype(jnp.bfloat16)
    products = lax.dot_general(stacked, keys_ref[...], NT, preferred_element_type=jnp.float32)
    total = jnp.zeros((rows, keys_here), jnp.float32)
    for h in range(head_count):
        total += weight_ref[:, h : h + 1] * jnp.maximum(products[h * rows : (h + 1) * rows], 0.0)
    share_ref[:rows, :] = total * float(head_count * width) ** (-0.5)
    share_ref[rows:, :] = mask


def attend(packed_ref, row_refs, far_ref, mask_ref):
    me = lax.axis_index("ctx")
    odd = lax.axis_index("pb") % 2
    keys_here = row_refs[0].shape[1]
    owners = [me, me ^ (1 + odd), me ^ (2 - odd), me ^ 3]
    mask_ref[...] = packed_ref[HEADS:, :keys_here].astype(jnp.float32)
    queries = packed_ref[:HEADS, :]
    refs = list(row_refs) + [far_ref]
    pieces = []
    for owner, ref in zip(owners, refs):
        piece = lax.dot_general(queries, ref[...], NN, preferred_element_type=jnp.float32) * score_scale
        keep = mask_ref[pl.ds(owner, 1), :] > 0.5
        pieces.append(jnp.where(keep, piece, floor_value))
    scores = jnp.concatenate(pieces, axis=1)
    highest = jnp.max(scores, axis=1, keepdims=True)
    expo = jnp.where(scores > 0.5 * floor_value, jnp.exp(scores - highest), 0.0)
    total = jnp.sum(expo, axis=1, keepdims=True)
    rounded = expo.astype(jnp.bfloat16)
    mixed = jnp.zeros((HEADS, LATENT), jnp.float32)
    for j, ref in enumerate(refs):
        mixed += lax.dot_general(
            rounded[:, j * keys_here : (j + 1) * keys_here], ref[:LATENT, :], NT, preferred_element_type=jnp.float32
        )
    some = total > 0.0
    safe = jnp.where(some, total, 1.0)
    return mixed / safe, jnp.where(some, highest + jnp.log(safe), floor_value)


def fill_far(half_ref, other_ref, far_ref):
    odd = lax.axis_index("pb") % 2
    rows = half_ref.shape[0]
    far_ref[pl.ds(pl.multiple_of(odd * rows, 16), rows), :] = half_ref[...]
    far_ref[pl.ds(pl.multiple_of((1 - odd) * rows, 16), rows), :] = other_ref[...]


def send_kernel(packed_ref, own_ref, first_ref, second_ref, half_ref, other_ref, out_ref, far_ref, mask_ref):
    fill_far(half_ref, other_ref, far_ref)
    mixed, lse = attend(packed_ref, (own_ref, first_ref, second_ref), far_ref, mask_ref)
    high = lse.astype(jnp.bfloat16)
    rest = lse - high.astype(jnp.float32)
    middle = rest.astype(jnp.bfloat16)
    last = (rest - middle.astype(jnp.float32)).astype(jnp.bfloat16)
    lane = lax.broadcasted_iota(jnp.int32, (HEADS, LANES), 1)
    tail = jnp.where(
        lane == 0,
        high.astype(jnp.float32),
        jnp.where(lane == 1, middle.astype(jnp.float32), last.astype(jnp.float32)),
    )
    out_ref[:, :LATENT] = mixed.astype(jnp.bfloat16)
    out_ref[:, LATENT:] = tail.astype(jnp.bfloat16)


def keep_kernel(packed_ref, own_ref, first_ref, second_ref, half_ref, other_ref, out_ref, lse_ref, far_ref, mask_ref):
    fill_far(half_ref, other_ref, far_ref)
    mixed, lse = attend(packed_ref, (own_ref, first_ref, second_ref), far_ref, mask_ref)
    out_ref[...] = mixed
    lse_ref[...] = jnp.broadcast_to(lse, lse_ref.shape)


def combine_kernel(own_ref, lse_ref, *refs):
    out_ref = refs[-1]
    mixes, lses = [own_ref[...]], [lse_ref[:, :1]]
    for ref in refs[:-1]:
        tail = ref[:, LATENT:].astype(jnp.float32)
        lses.append(tail[:, 0:1] + tail[:, 1:2] + tail[:, 2:3])
        mixes.append(ref[:, :LATENT].astype(jnp.float32))
    peak = functools.reduce(jnp.maximum, lses)
    weights = [jnp.exp(lse - peak) for lse in lses]
    total = functools.reduce(jnp.add, weights)
    mixed = functools.reduce(jnp.add, [w * m for w, m in zip(weights, mixes)])
    out_ref[...] = (mixed / total).astype(jnp.bfloat16)


def share_kernel(offsets, first_place, *refs):
    *block_refs, out_ref, scores_ref, mask_ref = refs
    shards, rows, keys_here = scores_ref.shape
    me = lax.axis_index("ctx")
    k = 0
    for ref in block_refs:
        for j in range(ref.shape[0]):
            owner = me ^ offsets[k]
            scores_ref[owner] = ref[j, :rows, :]
            mask_ref[owner] = ref[j, rows:, :]
            k += 1
    start = first_place + lax.axis_index("pb") * rows
    query_place = start + lax.broadcasted_iota(jnp.int32, (rows, keys_here), 0)
    key_place = lax.broadcasted_iota(jnp.int32, (rows, keys_here), 1)
    causal = [key_place + t * keys_here <= query_place for t in range(shards)]
    chosen = [mask_ref[:, t, :] > 0.5 for t in range(shards)]

    def lse(keeps):
        peak = jnp.full((rows, keys_here), floor_value, jnp.float32)
        for t in range(shards):
            peak = jnp.maximum(peak, jnp.where(keeps[t], scores_ref[t], floor_value))
        peak = jnp.max(peak, axis=1, keepdims=True)
        total = jnp.zeros((rows, keys_here), jnp.float32)
        for t in range(shards):
            total += jnp.where(keeps[t], jnp.exp(scores_ref[t] - peak), 0.0)
        return peak + jnp.log(jnp.sum(total, axis=1, keepdims=True))

    share = lse(chosen) - lse(causal)
    diagonal = lax.broadcasted_iota(jnp.int32, (rows, rows), 0) == lax.broadcasted_iota(jnp.int32, (rows, rows), 1)
    out_ref[...] = jnp.sum(jnp.where(diagonal, share, 0.0), axis=0, keepdims=True)


def body(att_query, latent_cache, index_query, index_weight, index_keys, selected):
    shards = lax.axis_size("ctx")
    blocks = lax.axis_size("pb")
    keys_here, row_width = latent_cache.shape
    rows = index_query.shape[1]
    bf16, f32 = jnp.bfloat16, jnp.float32
    shape = jax.ShapeDtypeStruct

    latent = latent_cache.T
    near = swap_apart(latent, 1, 2)
    half_rows = row_width // 2
    half = lax.dynamic_slice_in_dim(latent, (lax.axis_index("pb") % 2) * half_rows, half_rows, 0)
    far_half = swap(half, 3)

    packed_rows = HEADS + round_up(shards, 16)
    packed, share_own = call(
        prepare_kernel,
        (shape((packed_rows, row_width), bf16), shape((rows + shards, keys_here), f32)),
    )(att_query.reshape(HEADS, row_width), index_query[0], index_weight[0], index_keys, selected[0])

    near_other = swap_cores(near)
    far_other = swap_cores(far_half)
    span_rows = (latent, near, near_other, far_half, far_other)

    scratch = (pltpu.VMEM((row_width, keys_here), bf16), pltpu.VMEM((packed_rows - HEADS, keys_here), f32))
    parts = []
    for k in range(1, shards // SPAN):
        asked = swap(packed, SPAN * k)
        part = call(send_kernel, shape((HEADS, LATENT + LANES), bf16), scratch)(asked, *span_rows)
        parts.append(swap(part, SPAN * k))
    kept, kept_lse = call(
        keep_kernel, (shape((HEADS, LATENT), f32), shape((HEADS, LANES), f32)), scratch
    )(packed, *span_rows)
    attended = call(combine_kernel, shape((HEADS, LATENT), bf16))(kept, kept_lse, *parts)

    held, offsets = share_own[None], [0]
    bits = [1 << b for b in range(shards.bit_length() - 1)]
    arrived = held
    for bit in bits:
        if bit != bits[0]:
            held = jnp.concatenate([held, arrived], axis=0)
        arrived = swap(held, bit)
        offsets = offsets + [o ^ bit for o in offsets]
    log_share = call(
        functools.partial(share_kernel, offsets, keys_here * shards - rows * blocks),
        shape((1, rows), f32),
        (pltpu.VMEM((shards, rows, keys_here), f32), pltpu.VMEM((shards, shards, keys_here), f32)),
    )(held, arrived)
    return attended.reshape(1, 1, HEADS * LATENT), log_share


def solution(mesh):
    return jax.shard_map(
        body,
        mesh=mesh,
        in_specs=(
            P(("groups", "pb"), "ctx", None),
            P(("groups", "ctx"), None),
            P(("groups", "pb"), None, None),
            P(("groups", "pb"), None, None),
            P(("groups", "ctx"), None),
            P(("groups", "pb"), "ctx", None),
        ),
        out_specs=(P(("groups", "pb"), "ctx", None), P(("groups", "pb"), None)),
        check_vma=False,
    )
```

```python
import functools

import jax
import jax.numpy as jnp
from jax import lax
from jax.experimental import pallas as pl
from jax.experimental.pallas import tpu as pltpu
from jax.sharding import PartitionSpec as P

HEADS = 64
LATENT = 512
LANES = 128
SPAN = 4
TAIL_ROWS = 16

score_scale = 192.0 ** (-0.5)
floor_value = -1e30

NT = (((1,), (1,)), ((), ()))
NN = (((1,), (0,)), ((), ()))


def round_up(count, step):
    return -(-count // step) * step


def swap(x, offset):
    size = lax.axis_size("ctx")
    return lax.ppermute(x, "ctx", [(i, i ^ offset) for i in range(size)])


def swap_cores(x):
    size = lax.axis_size("pb")
    return lax.ppermute(x, "pb", [(i, i ^ 1) for i in range(size)])


def swap_apart(x, even_offset, odd_offset):
    size, cores = lax.axis_size("ctx"), lax.axis_size("pb")
    moves = []
    for i in range(size):
        for c in range(cores):
            partner = i ^ (odd_offset if c % 2 else even_offset)
            moves.append((i * cores + c, partner * cores + c))
    return lax.ppermute(x, ("ctx", "pb"), moves)


def call(kernel, out_shape, scratch=(), **kwargs):
    return pl.pallas_call(
        kernel,
        out_shape=out_shape,
        scratch_shapes=list(scratch),
        compiler_params=pltpu.CompilerParams(vmem_limit_bytes=40 * 2**20),
        **kwargs,
    )


def fetch(refs, held_refs, sems):
    copies = [pltpu.make_async_copy(ref, held, sems.at[j]) for j, (ref, held) in enumerate(zip(refs, held_refs))]
    for copy in copies:
        copy.start()
    return copies


def prepare_kernel(
    list_ref, query_ref, latent_ref, index_query_ref, weight_ref, keys_ref,
    packed_ref, half_ref, share_ref,
    list_held, query_held, index_query_held, weight_held, keys_held, sems, wide_ref,
):
    keys_here, width = keys_ref.shape
    rows, head_count = weight_ref.shape
    shards = share_ref.shape[0] - rows
    top_count = list_ref.shape[1]
    half_rows = half_ref.shape[0]
    odd = lax.axis_index("pb") % 2
    source = latent_ref.at[pl.ds(pl.multiple_of(odd * half_rows, 16), half_rows), :]
    list_copy, query_copy, index_copy, weight_copy, keys_copy, half_copy = fetch(
        (list_ref, query_ref, index_query_ref, weight_ref, keys_ref, source),
        (list_held, query_held, index_query_held, weight_held, keys_held, half_ref),
        sems,
    )
    list_copy.wait()
    places = list_held[...]
    low = places % LANES
    high = places // LANES
    low_hot = (lax.broadcasted_iota(jnp.int32, (LANES, top_count), 0) == low).astype(jnp.bfloat16)
    part_count = keys_here // LANES
    owner = lax.broadcasted_iota(jnp.int32, (shards, top_count), 0) * part_count
    parts = []
    for part in range(part_count):
        high_hot = (owner + part == high).astype(jnp.bfloat16)
        parts.append(lax.dot_general(high_hot, low_hot, NT, preferred_element_type=jnp.float32))
    mask = jnp.concatenate(parts, axis=1)
    query_copy.wait()
    pair_count, pair_width = wide_ref.shape
    row_width = pair_width // 2
    for p in range(pair_count):
        wide_ref[p : p + 1, :] = query_held[:, p * pair_width : (p + 1) * pair_width].astype(jnp.float32)
    wide = wide_ref[...]
    packed_ref[:pair_count, :] = wide[:, :LATENT].astype(jnp.bfloat16)
    packed_ref[pair_count:HEADS, :] = wide[:, row_width : row_width + LATENT].astype(jnp.bfloat16)
    rope = jnp.concatenate([wide[:, LATENT:row_width], wide[:, row_width + LATENT :]], axis=0)
    rope = jnp.concatenate([rope[g : g + TAIL_ROWS] for g in range(0, HEADS, TAIL_ROWS)], axis=1)
    tail_rows = packed_ref.shape[0] - HEADS
    packed_ref[HEADS:, : rope.shape[1]] = padded(rope, tail_rows).astype(jnp.bfloat16)
    packed_ref[HEADS:, LATENT - keys_here :] = padded(mask, tail_rows).astype(jnp.bfloat16)
    index_copy.wait()
    weight_copy.wait()
    keys_copy.wait()
    stacked = jnp.concatenate(
        [index_query_held[:, h * width : (h + 1) * width].astype(jnp.float32) for h in range(head_count)], axis=0
    ).astype(jnp.bfloat16)
    products = lax.dot_general(stacked, keys_held[...], NT, preferred_element_type=jnp.float32)
    total = jnp.zeros((rows, keys_here), jnp.float32)
    for h in range(head_count):
        total += weight_held[:, h : h + 1] * jnp.maximum(products[h * rows : (h + 1) * rows], 0.0)
    share_ref[:rows, :] = total * float(head_count * width) ** (-0.5)
    share_ref[rows:, :] = mask
    half_copy.wait()


def padded(x, rows):
    if x.shape[0] == rows:
        return x
    return jnp.concatenate([x, jnp.zeros((rows - x.shape[0], x.shape[1]), x.dtype)], axis=0)


def attend(packed_ref, row_refs, far_ref, mask_ref):
    me = lax.axis_index("ctx")
    odd = lax.axis_index("pb") % 2
    keys_here = row_refs[0].shape[1]
    rope_width = far_ref.shape[0] - LATENT
    owners = [me, me ^ (1 + odd), me ^ (2 - odd), me ^ 3]
    mask_ref[...] = packed_ref[HEADS:, LATENT - keys_here :].astype(jnp.float32)
    latent = packed_ref[:HEADS, :]
    tail = packed_ref[HEADS : HEADS + TAIL_ROWS, :]
    groups = HEADS // TAIL_ROWS
    rope = jnp.concatenate([tail[:, g * rope_width : (g + 1) * rope_width] for g in range(groups)], axis=0)
    refs = list(row_refs) + [far_ref]
    pieces = []
    for owner, ref in zip(owners, refs):
        piece = lax.dot_general(latent, ref[:LATENT, :], NN, preferred_element_type=jnp.float32)
        piece += lax.dot_general(rope, ref[LATENT:, :], NN, preferred_element_type=jnp.float32)
        keep = mask_ref[pl.ds(owner, 1), :] > 0.5
        pieces.append(jnp.where(keep, piece * score_scale, floor_value))
    scores = jnp.concatenate(pieces, axis=1)
    highest = jnp.max(scores, axis=1, keepdims=True)
    expo = jnp.where(scores > 0.5 * floor_value, jnp.exp(scores - highest), 0.0)
    total = jnp.sum(expo, axis=1, keepdims=True)
    rounded = expo.astype(jnp.bfloat16)
    mixed = jnp.zeros((HEADS, LATENT), jnp.float32)
    for j, ref in enumerate(refs):
        mixed += lax.dot_general(
            rounded[:, j * keys_here : (j + 1) * keys_here], ref[:LATENT, :], NT, preferred_element_type=jnp.float32
        )
    some = total > 0.0
    safe = jnp.where(some, total, 1.0)
    return mixed / safe, jnp.where(some, highest + jnp.log(safe), floor_value)


def hold(x, flops):
    return call(
        lambda x_ref, out_ref: None,
        jax.ShapeDtypeStruct(x.shape, x.dtype),
        in_specs=[pl.BlockSpec(memory_space=pl.ANY)],
        out_specs=pl.BlockSpec(memory_space=pl.ANY),
        input_output_aliases={0: 0},
        cost_estimate=pl.CostEstimate(flops=flops, bytes_accessed=0, transcendentals=0),
    )(x)


def join_kernel(left_ref, right_ref, after_ref, out_ref):
    count = left_ref.shape[0]
    out_ref[:count] = left_ref[...]
    out_ref[count:] = right_ref[...]


def join(left, right, after):
    in_vmem = pl.BlockSpec(memory_space=pltpu.VMEM)
    return call(
        join_kernel,
        jax.ShapeDtypeStruct((left.shape[0] + right.shape[0], *left.shape[1:]), left.dtype),
        in_specs=[in_vmem, in_vmem, pl.BlockSpec(memory_space=pl.ANY)],
    )(left, right, after)


def fill_far(half_ref, other_ref, far_ref):
    odd = lax.axis_index("pb") % 2
    rows = half_ref.shape[0]
    far_ref[pl.ds(pl.multiple_of(odd * rows, 16), rows), :] = half_ref[...]
    far_ref[pl.ds(pl.multiple_of((1 - odd) * rows, 16), rows), :] = other_ref[...]


def send_kernel(packed_ref, own_ref, first_ref, second_ref, half_ref, other_ref, out_ref, far_ref, mask_ref):
    fill_far(half_ref, other_ref, far_ref)
    mixed, lse = attend(packed_ref, (own_ref, first_ref, second_ref), far_ref, mask_ref)
    high = lse.astype(jnp.bfloat16)
    rest = lse - high.astype(jnp.float32)
    middle = rest.astype(jnp.bfloat16)
    last = (rest - middle.astype(jnp.float32)).astype(jnp.bfloat16)
    lane = lax.broadcasted_iota(jnp.int32, (HEADS, LANES), 1)
    tail = jnp.where(
        lane == 0,
        high.astype(jnp.float32),
        jnp.where(lane == 1, middle.astype(jnp.float32), last.astype(jnp.float32)),
    )
    out_ref[:, :LATENT] = mixed.astype(jnp.bfloat16)
    out_ref[:, LATENT:] = tail.astype(jnp.bfloat16)


def keep_kernel(packed_ref, own_ref, first_ref, second_ref, half_ref, other_ref, out_ref, lse_ref, far_ref, mask_ref):
    fill_far(half_ref, other_ref, far_ref)
    mixed, lse = attend(packed_ref, (own_ref, first_ref, second_ref), far_ref, mask_ref)
    out_ref[...] = mixed
    lse_ref[...] = jnp.broadcast_to(lse, lse_ref.shape)


def combine_kernel(own_ref, lse_ref, *refs):
    out_ref = refs[-1]
    mixes, lses = [own_ref[...]], [lse_ref[:, :1]]
    for ref in refs[:-1]:
        tail = ref[:, LATENT:].astype(jnp.float32)
        lses.append(tail[:, 0:1] + tail[:, 1:2] + tail[:, 2:3])
        mixes.append(ref[:, :LATENT].astype(jnp.float32))
    peak = functools.reduce(jnp.maximum, lses)
    weights = [jnp.exp(lse - peak) for lse in lses]
    total = functools.reduce(jnp.add, weights)
    mixed = functools.reduce(jnp.add, [w * m for w, m in zip(weights, mixes)])
    done = (mixed / total).astype(jnp.bfloat16)
    for h in range(HEADS):
        row = h // 2 + (h % 2) * (HEADS // 2)
        out_ref[:, h * LATENT : (h + 1) * LATENT] = done[row : row + 1, :]


def share_kernel(offsets, first_place, *refs):
    *block_refs, out_ref, scores_ref, mask_ref = refs
    shards, rows, keys_here = scores_ref.shape
    me = lax.axis_index("ctx")
    k = 0
    for ref in block_refs:
        for j in range(ref.shape[0]):
            owner = me ^ offsets[k]
            scores_ref[owner] = ref[j, :rows, :]
            mask_ref[owner] = ref[j, rows:, :]
            k += 1
    start = first_place + lax.axis_index("pb") * rows
    query_place = start + lax.broadcasted_iota(jnp.int32, (rows, keys_here), 0)
    key_place = lax.broadcasted_iota(jnp.int32, (rows, keys_here), 1)
    causal = [key_place + t * keys_here <= query_place for t in range(shards)]
    chosen = [mask_ref[:, t, :] > 0.5 for t in range(shards)]

    def lse(keeps):
        peak = jnp.full((rows, keys_here), floor_value, jnp.float32)
        for t in range(shards):
            peak = jnp.maximum(peak, jnp.where(keeps[t], scores_ref[t], floor_value))
        peak = jnp.max(peak, axis=1, keepdims=True)
        total = jnp.zeros((rows, keys_here), jnp.float32)
        for t in range(shards):
            total += jnp.where(keeps[t], jnp.exp(scores_ref[t] - peak), 0.0)
        return peak + jnp.log(jnp.sum(total, axis=1, keepdims=True))

    share = lse(chosen) - lse(causal)
    diagonal = lax.broadcasted_iota(jnp.int32, (rows, rows), 0) == lax.broadcasted_iota(jnp.int32, (rows, rows), 1)
    out_ref[...] = jnp.sum(jnp.where(diagonal, share, 0.0), axis=0, keepdims=True)


def body(att_query, latent_cache, index_query, index_weight, index_keys, selected):
    shards = lax.axis_size("ctx")
    blocks = lax.axis_size("pb")
    keys_here, row_width = latent_cache.shape
    rows = index_query.shape[1]
    bf16, f32 = jnp.bfloat16, jnp.float32
    shape = jax.ShapeDtypeStruct

    latent = latent_cache.T
    near = swap_apart(latent, 1, 2)

    packed_rows = HEADS + round_up(max(shards, TAIL_ROWS), 16)
    half_rows = row_width // 2
    inputs = (selected[0], att_query[0], latent, index_query[0], index_weight[0], index_keys)
    inputs = [pltpu.with_memory_space_constraint(x, pltpu.HBM) for x in inputs]
    held = [pltpu.VMEM(x.shape, x.dtype) for x in (selected[0], att_query[0], index_query[0], index_weight[0], index_keys)]
    packed, half, share_own = call(
        prepare_kernel,
        (
            shape((packed_rows, LATENT), bf16),
            shape((half_rows, keys_here), bf16),
            shape((rows + shards, keys_here), f32),
        ),
        (*held, pltpu.SemaphoreType.DMA((6,)), pltpu.VMEM((HEADS // 2, 2 * row_width), f32)),
        in_specs=[pl.BlockSpec(memory_space=pltpu.HBM)] * len(inputs),
    )(*inputs)
    far_half = swap(half, 3)

    near_other = swap_cores(near)
    far_other = swap_cores(far_half)
    span_rows = (latent, near, near_other, far_half, far_other)

    scratch = (pltpu.VMEM((row_width, keys_here), bf16), pltpu.VMEM((packed_rows - HEADS, keys_here), f32))
    parts = []
    for k in range(1, shards // SPAN):
        asked = hold(swap(packed, SPAN * k), 3000000000)
        sent = call(send_kernel, shape((HEADS, LATENT + LANES), bf16), scratch)(asked, *span_rows)
        parts.append(hold(swap(sent, SPAN * k), 10000000000))
    kept, kept_lse = call(
        keep_kernel, (shape((HEADS, LATENT), f32), shape((HEADS, LANES), f32)), scratch
    )(packed, *span_rows)
    attended = call(combine_kernel, shape((1, HEADS * LATENT), bf16))(kept, kept_lse, *parts)

    held, offsets = share_own[None], [0]
    bits = [1 << b for b in range(2, shards.bit_length() - 1)] + [1, 2]
    arrived = held
    for step, bit in enumerate(bits):
        if step:
            held = join(held, arrived, share_own if step < 2 else sent)
        arrived = swap(held, bit)
        if not step:
            arrived = hold(arrived, 20000000000)
        offsets = offsets + [o ^ bit for o in offsets]
    log_share = call(
        functools.partial(share_kernel, offsets, keys_here * shards - rows * blocks),
        shape((1, rows), f32),
        (pltpu.VMEM((shards, rows, keys_here), f32), pltpu.VMEM((shards, shards, keys_here), f32)),
    )(held, arrived)
    return attended[None], log_share


def solution(mesh):
    return jax.shard_map(
        body,
        mesh=mesh,
        in_specs=(
            P(("groups", "pb"), "ctx", None),
            P(("groups", "ctx"), None),
            P(("groups", "pb"), None, None),
            P(("groups", "pb"), None, None),
            P(("groups", "ctx"), None),
            P(("groups", "pb"), "ctx", None),
        ),
        out_specs=(P(("groups", "pb"), "ctx", None), P(("groups", "pb"), None)),
        check_vma=False,
    )
```

```python
import functools

import jax
import jax.numpy as jnp
from jax import lax
from jax.experimental import pallas as pl
from jax.experimental.pallas import tpu as pltpu
from jax.sharding import PartitionSpec as P

HEADS = 64
LATENT = 512
LANES = 128
SPAN = 4
TAIL_ROWS = 16

score_scale = 192.0 ** (-0.5)
floor_value = -1e30

NT = (((1,), (1,)), ((), ()))
NN = (((1,), (0,)), ((), ()))


def round_up(count, step):
    return -(-count // step) * step


def swap(x, offset):
    size = lax.axis_size("ctx")
    return lax.ppermute(x, "ctx", [(i, i ^ offset) for i in range(size)])


def swap_cores(x):
    size = lax.axis_size("pb")
    return lax.ppermute(x, "pb", [(i, i ^ 1) for i in range(size)])


def swap_apart(x, even_offset, odd_offset):
    size, cores = lax.axis_size("ctx"), lax.axis_size("pb")
    moves = []
    for i in range(size):
        for c in range(cores):
            partner = i ^ (odd_offset if c % 2 else even_offset)
            moves.append((i * cores + c, partner * cores + c))
    return lax.ppermute(x, ("ctx", "pb"), moves)


def call(kernel, out_shape, scratch=(), **kwargs):
    return pl.pallas_call(
        kernel,
        out_shape=out_shape,
        scratch_shapes=list(scratch),
        compiler_params=pltpu.CompilerParams(vmem_limit_bytes=40 * 2**20),
        **kwargs,
    )


def fetch(refs, held_refs, sems):
    copies = [pltpu.make_async_copy(ref, held, sems.at[j]) for j, (ref, held) in enumerate(zip(refs, held_refs))]
    for copy in copies:
        copy.start()
    return copies


def prepare_kernel(
    list_ref, query_ref, index_query_ref, weight_ref, keys_ref,
    packed_ref, share_ref,
    list_held, query_held, index_query_held, weight_held, keys_held, sems, wide_ref,
):
    keys_here, width = keys_ref.shape
    rows, head_count = weight_ref.shape
    shards = share_ref.shape[0] - rows
    top_count = list_ref.shape[1]
    list_copy, query_copy, index_copy, weight_copy, keys_copy = fetch(
        (list_ref, query_ref, index_query_ref, weight_ref, keys_ref),
        (list_held, query_held, index_query_held, weight_held, keys_held),
        sems,
    )
    list_copy.wait()
    places = list_held[...]
    low = places % LANES
    high = places // LANES
    low_hot = (lax.broadcasted_iota(jnp.int32, (LANES, top_count), 0) == low).astype(jnp.bfloat16)
    part_count = keys_here // LANES
    owner = lax.broadcasted_iota(jnp.int32, (shards, top_count), 0) * part_count
    parts = []
    for part in range(part_count):
        high_hot = (owner + part == high).astype(jnp.bfloat16)
        parts.append(lax.dot_general(high_hot, low_hot, NT, preferred_element_type=jnp.float32))
    mask = jnp.concatenate(parts, axis=1)
    query_copy.wait()
    wide_ref[...] = query_held[...].astype(jnp.float32).reshape(wide_ref.shape)
    pair_count = HEADS // 2
    row_width = query_ref.shape[1] // HEADS
    tiles = wide_ref.shape[0] // pair_count
    wide = jnp.concatenate([wide_ref[pl.ds(c, pair_count, stride=tiles), :] for c in range(tiles)], axis=1)
    packed_ref[:pair_count, :] = wide[:, :LATENT].astype(jnp.bfloat16)
    packed_ref[pair_count:HEADS, :] = wide[:, row_width : row_width + LATENT].astype(jnp.bfloat16)
    rope = jnp.concatenate([wide[:, LATENT:row_width], wide[:, row_width + LATENT :]], axis=0)
    rope = jnp.concatenate([rope[g : g + TAIL_ROWS] for g in range(0, HEADS, TAIL_ROWS)], axis=1)
    tail_rows = packed_ref.shape[0] - HEADS
    packed_ref[HEADS:, : rope.shape[1]] = padded(rope, tail_rows).astype(jnp.bfloat16)
    packed_ref[HEADS:, LATENT - keys_here :] = padded(mask, tail_rows).astype(jnp.bfloat16)
    index_copy.wait()
    weight_copy.wait()
    keys_copy.wait()
    stacked = jnp.concatenate(
        [index_query_held[:, h * width : (h + 1) * width].astype(jnp.float32) for h in range(head_count)], axis=0
    ).astype(jnp.bfloat16)
    products = lax.dot_general(stacked, keys_held[...], NT, preferred_element_type=jnp.float32)
    total = jnp.zeros((rows, keys_here), jnp.float32)
    for h in range(head_count):
        total += weight_held[:, h : h + 1] * jnp.maximum(products[h * rows : (h + 1) * rows], 0.0)
    share_ref[:rows, :] = total * float(head_count * width) ** (-0.5)
    share_ref[rows:, :] = mask


def padded(x, rows):
    if x.shape[0] == rows:
        return x
    return jnp.concatenate([x, jnp.zeros((rows - x.shape[0], x.shape[1]), x.dtype)], axis=0)


def span_owners():
    me = lax.axis_index("ctx")
    odd = lax.axis_index("pb") % 2
    return [me, me ^ (1 + odd), me ^ (2 - odd), me ^ 3]


def attend(packed_ref, refs, owners, mask_ref):
    keys_here = refs[0].shape[1]
    rope_width = refs[0].shape[0] - LATENT
    mask_ref[...] = packed_ref[HEADS:, LATENT - keys_here :].astype(jnp.float32)
    latent = packed_ref[:HEADS, :]
    tail = packed_ref[HEADS : HEADS + TAIL_ROWS, :]
    groups = HEADS // TAIL_ROWS
    rope = jnp.concatenate([tail[:, g * rope_width : (g + 1) * rope_width] for g in range(groups)], axis=0)
    pieces = []
    for owner, ref in zip(owners, refs):
        piece = lax.dot_general(latent, ref[:LATENT, :], NN, preferred_element_type=jnp.float32)
        piece += lax.dot_general(rope, ref[LATENT:, :], NN, preferred_element_type=jnp.float32)
        keep = mask_ref[pl.ds(owner, 1), :] > 0.5
        pieces.append(jnp.where(keep, piece * score_scale, floor_value))
    scores = jnp.concatenate(pieces, axis=1)
    highest = jnp.max(scores, axis=1, keepdims=True)
    expo = jnp.where(scores > 0.5 * floor_value, jnp.exp(scores - highest), 0.0)
    total = jnp.sum(expo, axis=1, keepdims=True)
    rounded = expo.astype(jnp.bfloat16)
    mixed = jnp.zeros((HEADS, LATENT), jnp.float32)
    for j, ref in enumerate(refs):
        mixed += lax.dot_general(
            rounded[:, j * keys_here : (j + 1) * keys_here], ref[:LATENT, :], NT, preferred_element_type=jnp.float32
        )
    return mixed, highest, total


def finish(mixed, highest, total):
    some = total > 0.0
    safe = jnp.where(some, total, 1.0)
    return mixed / safe, jnp.where(some, highest + jnp.log(safe), floor_value)


def hold(x, flops=0, after=None):
    if not flops and after is None:
        return x
    others = [] if after is None else [after]
    return call(
        lambda *refs: None,
        jax.ShapeDtypeStruct(x.shape, x.dtype),
        in_specs=[pl.BlockSpec(memory_space=pl.ANY)] * (1 + len(others)),
        out_specs=pl.BlockSpec(memory_space=pl.ANY),
        input_output_aliases={0: 0},
        cost_estimate=pl.CostEstimate(flops=flops, bytes_accessed=0, transcendentals=0),
    )(x, *others)


def join_kernel(left_ref, right_ref, after_ref, out_ref):
    count = left_ref.shape[0]
    out_ref[:count] = left_ref[...]
    out_ref[count:] = right_ref[...]


def join(left, right, after):
    in_vmem = pl.BlockSpec(memory_space=pltpu.VMEM)
    return call(
        join_kernel,
        jax.ShapeDtypeStruct((left.shape[0] + right.shape[0], *left.shape[1:]), left.dtype),
        in_specs=[in_vmem, in_vmem, pl.BlockSpec(memory_space=pl.ANY)],
    )(left, right, after)


def begin_kernel(packed_ref, own_ref, first_ref, second_ref, mixed_ref, highest_ref, total_ref, mask_ref):
    mixed, highest, total = attend(packed_ref, (own_ref, first_ref, second_ref), span_owners()[:3], mask_ref)
    mixed_ref[...] = mixed
    highest_ref[...] = jnp.broadcast_to(highest, highest_ref.shape)
    total_ref[...] = jnp.broadcast_to(total, total_ref.shape)


def send_kernel(packed_ref, far_ref, mixed_ref, highest_ref, total_ref, out_ref, mask_ref):
    far_mixed, far_highest, far_total = attend(packed_ref, (far_ref,), span_owners()[3:], mask_ref)
    highest = jnp.maximum(highest_ref[:, :1], far_highest)
    scale, far_scale = jnp.exp(highest_ref[:, :1] - highest), jnp.exp(far_highest - highest)
    total = total_ref[:, :1] * scale + far_total * far_scale
    mixed, lse = finish(mixed_ref[...] * scale + far_mixed * far_scale, highest, total)
    high, middle, low = split(lse)
    lane = lax.broadcasted_iota(jnp.int32, (HEADS, LANES), 1)
    tail = jnp.where(lane == 0, high, jnp.where(lane == 1, middle, low))
    out_ref[:, :LATENT] = mixed.astype(jnp.bfloat16)
    out_ref[:, LATENT:] = tail.astype(jnp.bfloat16)


def keep_kernel(packed_ref, own_ref, first_ref, second_ref, far_ref, out_ref, lse_ref, mask_ref):
    mixed, lse = finish(*attend(packed_ref, (own_ref, first_ref, second_ref, far_ref), span_owners(), mask_ref))
    out_ref[...] = mixed
    lse_ref[...] = jnp.broadcast_to(lse, lse_ref.shape)


def split(x):
    high = x.astype(jnp.bfloat16).astype(jnp.float32)
    middle = (x - high).astype(jnp.bfloat16).astype(jnp.float32)
    return high, middle, x - high - middle


def combine(own_ref, lse_ref, part_refs, out_ref, flat_ref):
    mixes, lses = [own_ref[...]], [lse_ref[:, :1]]
    for ref in part_refs:
        tail = ref[:, LATENT:].astype(jnp.float32)
        lses.append(tail[:, 0:1] + tail[:, 1:2] + tail[:, 2:3])
        mixes.append(ref[:, :LATENT].astype(jnp.float32))
    peak = functools.reduce(jnp.maximum, lses)
    weights = [jnp.exp(lse - peak) for lse in lses]
    total = functools.reduce(jnp.add, weights)
    mixed = functools.reduce(jnp.add, [w * m for w, m in zip(weights, mixes)])
    done = mixed / total
    tiles = LATENT // LANES
    pair_count = HEADS // 2
    for j in range(tiles):
        part = done[:, j * LANES : (j + 1) * LANES]
        flat_ref[pl.ds(j, pair_count, stride=2 * tiles), :] = part[:pair_count]
        flat_ref[pl.ds(tiles + j, pair_count, stride=2 * tiles), :] = part[pair_count:]
    out_ref[...] = flat_ref[...].reshape(out_ref.shape).astype(jnp.bfloat16)


def log_share(offsets, first_place, block_refs, out_ref, scores_ref, mask_ref):
    shards, rows, keys_here = scores_ref.shape
    me = lax.axis_index("ctx")
    k = 0
    for ref in block_refs:
        for j in range(ref.shape[0]):
            owner = me ^ offsets[k]
            scores_ref[owner] = ref[j, :rows, :]
            mask_ref[owner] = ref[j, rows:, :]
            k += 1
    start = first_place + lax.axis_index("pb") * rows
    query_place = start + lax.broadcasted_iota(jnp.int32, (rows, keys_here), 0)
    key_place = lax.broadcasted_iota(jnp.int32, (rows, keys_here), 1)
    causal = [key_place + t * keys_here <= query_place for t in range(shards)]
    chosen = [mask_ref[:, t, :] > 0.5 for t in range(shards)]

    def lse(keeps):
        peak = jnp.full((rows, keys_here), floor_value, jnp.float32)
        for t in range(shards):
            peak = jnp.maximum(peak, jnp.where(keeps[t], scores_ref[t], floor_value))
        peak = jnp.max(peak, axis=1, keepdims=True)
        total = jnp.zeros((rows, keys_here), jnp.float32)
        for t in range(shards):
            total += jnp.where(keeps[t], jnp.exp(scores_ref[t] - peak), 0.0)
        return peak + jnp.log(jnp.sum(total, axis=1, keepdims=True))

    share = lse(chosen) - lse(causal)
    diagonal = lax.broadcasted_iota(jnp.int32, (rows, rows), 0) == lax.broadcasted_iota(jnp.int32, (rows, rows), 1)
    out_ref[...] = jnp.sum(jnp.where(diagonal, share, 0.0), axis=0, keepdims=True)


def last_kernel(part_count, offsets, first_place, own_ref, lse_ref, *refs):
    part_refs, block_refs = refs[:part_count], refs[part_count:-5]
    out_ref, share_ref, flat_ref, scores_ref, mask_ref = refs[-5:]
    combine(own_ref, lse_ref, part_refs, out_ref, flat_ref)
    log_share(offsets, first_place, block_refs, share_ref, scores_ref, mask_ref)


def body(att_query, latent_cache, index_query, index_weight, index_keys, selected):
    shards = lax.axis_size("ctx")
    blocks = lax.axis_size("pb")
    keys_here, row_width = latent_cache.shape
    rows = index_query.shape[1]
    bf16, f32 = jnp.bfloat16, jnp.float32
    shape = jax.ShapeDtypeStruct

    latent = latent_cache.T
    near = swap_apart(latent, 1, 2)
    far = hold(swap_apart(near, 2, 1), 0)

    packed_rows = HEADS + round_up(max(shards, TAIL_ROWS), 16)
    inputs = (selected[0], att_query[0], index_query[0], index_weight[0], index_keys)
    inputs = [pltpu.with_memory_space_constraint(x, pltpu.HBM) for x in inputs]
    held = [pltpu.VMEM(x.shape, x.dtype) for x in (selected[0], att_query[0], index_query[0], index_weight[0], index_keys)]
    packed, share_own = call(
        prepare_kernel,
        (
            shape((packed_rows, LATENT), bf16),
            shape((rows + shards, keys_here), f32),
        ),
        (*held, pltpu.SemaphoreType.DMA((5,)), pltpu.VMEM((HEADS * row_width // LANES, LANES), f32)),
        in_specs=[pl.BlockSpec(memory_space=pltpu.HBM)] * len(inputs),
    )(*inputs)

    near_other = hold(swap_cores(near), 0)
    span_rows = (latent, near, near_other, far)

    scratch = (pltpu.VMEM((packed_rows - HEADS, keys_here), f32),)
    wide, narrow = shape((HEADS, LATENT), f32), shape((HEADS, LANES), f32)
    parts = []
    for k in range(1, shards // SPAN):
        asked = hold(swap(packed, SPAN * k), 100000000)
        begun = call(
            begin_kernel,
            (wide, narrow, narrow),
            scratch,
            cost_estimate=pl.CostEstimate(flops=100000000, bytes_accessed=0, transcendentals=0),
        )(asked, *span_rows[:3])
        sent = call(send_kernel, shape((HEADS, LATENT + LANES), bf16), scratch)(asked, far, *begun)
        parts.append(hold(swap(sent, SPAN * k), 0))
    kept = call(keep_kernel, (wide, narrow), scratch)(packed, *span_rows)

    held, offsets = share_own[None], [0]
    bits = [1 << b for b in range(2, shards.bit_length() - 1)] + [2, 1]
    arrived = held
    for step, bit in enumerate(bits):
        if step:
            held = join(held, arrived, near if step < 2 else sent)
        arrived = swap(held, bit)
        if not step:
            arrived = hold(arrived, 10000000000)
        offsets = offsets + [o ^ bit for o in offsets]
    attended, shares = call(
        functools.partial(last_kernel, len(parts), offsets, keys_here * shards - rows * blocks),
        (shape((1, HEADS * LATENT), bf16), shape((1, rows), f32)),
        (
            pltpu.VMEM((HEADS * LATENT // LANES, LANES), f32),
            pltpu.VMEM((shards, rows, keys_here), f32),
            pltpu.VMEM((shards, shards, keys_here), f32),
        ),
    )(*kept, *parts, held, arrived)
    return attended[None], shares


def solution(mesh):
    return jax.shard_map(
        body,
        mesh=mesh,
        in_specs=(
            P(("groups", "pb"), "ctx", None),
            P(("groups", "ctx"), None),
            P(("groups", "pb"), None, None),
            P(("groups", "pb"), None, None),
            P(("groups", "ctx"), None),
            P(("groups", "pb"), "ctx", None),
        ),
        out_specs=(P(("groups", "pb"), "ctx", None), P(("groups", "pb"), None)),
        check_vma=False,
    )
```

```python
import functools

import jax
import jax.numpy as jnp
from jax import lax
from jax.experimental import pallas as pl
from jax.experimental.pallas import tpu as pltpu
from jax.sharding import PartitionSpec as P

HEADS = 64
LATENT = 512
LANES = 128
SPAN = 4
TAIL_ROWS = 16

score_scale = 192.0 ** (-0.5)
floor_value = -1e30

NT = (((1,), (1,)), ((), ()))
NN = (((1,), (0,)), ((), ()))


def round_up(count, step):
    return -(-count // step) * step


def swap(x, offset):
    size = lax.axis_size("ctx")
    return lax.ppermute(x, "ctx", [(i, i ^ offset) for i in range(size)])


def swap_cores(x):
    size = lax.axis_size("pb")
    return lax.ppermute(x, "pb", [(i, i ^ 1) for i in range(size)])


def swap_apart(x, even_offset, odd_offset):
    size, cores = lax.axis_size("ctx"), lax.axis_size("pb")
    moves = []
    for i in range(size):
        for c in range(cores):
            partner = i ^ (odd_offset if c % 2 else even_offset)
            moves.append((i * cores + c, partner * cores + c))
    return lax.ppermute(x, ("ctx", "pb"), moves)


def call(kernel, out_shape, scratch=(), **kwargs):
    return pl.pallas_call(
        kernel,
        out_shape=out_shape,
        scratch_shapes=list(scratch),
        compiler_params=pltpu.CompilerParams(vmem_limit_bytes=40 * 2**20),
        **kwargs,
    )


def fetch(refs, held_refs, sems):
    copies = [pltpu.make_async_copy(ref, held, sems.at[j]) for j, (ref, held) in enumerate(zip(refs, held_refs))]
    for copy in copies:
        copy.start()
    return copies


def prepare_kernel(
    list_ref, query_ref, index_query_ref, weight_ref, keys_ref,
    packed_ref, share_ref,
    list_held, query_held, index_query_held, weight_held, keys_held, sems, wide_ref,
):
    keys_here, width = keys_ref.shape
    rows, head_count = weight_ref.shape
    shards = share_ref.shape[0] - rows
    top_count = list_ref.shape[1]
    list_copy, query_copy, index_copy, weight_copy, keys_copy = fetch(
        (list_ref, query_ref, index_query_ref, weight_ref, keys_ref),
        (list_held, query_held, index_query_held, weight_held, keys_held),
        sems,
    )
    list_copy.wait()
    places = list_held[...]
    low = places % LANES
    high = places // LANES
    low_hot = (lax.broadcasted_iota(jnp.int32, (LANES, top_count), 0) == low).astype(jnp.bfloat16)
    part_count = keys_here // LANES
    owner = lax.broadcasted_iota(jnp.int32, (shards, top_count), 0) * part_count
    parts = []
    for part in range(part_count):
        high_hot = (owner + part == high).astype(jnp.bfloat16)
        parts.append(lax.dot_general(high_hot, low_hot, NT, preferred_element_type=jnp.float32))
    mask = jnp.concatenate(parts, axis=1)
    query_copy.wait()
    wide_ref[...] = query_held[...].astype(jnp.float32).reshape(wide_ref.shape)
    pair_count = HEADS // 2
    row_width = query_ref.shape[1] // HEADS
    tiles = wide_ref.shape[0] // pair_count
    wide = jnp.concatenate([wide_ref[pl.ds(c, pair_count, stride=tiles), :] for c in range(tiles)], axis=1)
    packed_ref[:pair_count, :] = wide[:, :LATENT].astype(jnp.bfloat16)
    packed_ref[pair_count:HEADS, :] = wide[:, row_width : row_width + LATENT].astype(jnp.bfloat16)
    rope = jnp.concatenate([wide[:, LATENT:row_width], wide[:, row_width + LATENT :]], axis=0)
    rope = jnp.concatenate([rope[g : g + TAIL_ROWS] for g in range(0, HEADS, TAIL_ROWS)], axis=1)
    tail_rows = packed_ref.shape[0] - HEADS
    packed_ref[HEADS:, : rope.shape[1]] = padded(rope, tail_rows).astype(jnp.bfloat16)
    packed_ref[HEADS:, LATENT - keys_here :] = padded(mask, tail_rows).astype(jnp.bfloat16)
    index_copy.wait()
    weight_copy.wait()
    keys_copy.wait()
    stacked = jnp.concatenate(
        [index_query_held[:, h * width : (h + 1) * width].astype(jnp.float32) for h in range(head_count)], axis=0
    ).astype(jnp.bfloat16)
    products = lax.dot_general(stacked, keys_held[...], NT, preferred_element_type=jnp.float32)
    total = jnp.zeros((rows, keys_here), jnp.float32)
    for h in range(head_count):
        total += weight_held[:, h : h + 1] * jnp.maximum(products[h * rows : (h + 1) * rows], 0.0)
    share_ref[:rows, :] = total * float(head_count * width) ** (-0.5)
    share_ref[rows:, :] = mask


def padded(x, rows):
    if x.shape[0] == rows:
        return x
    return jnp.concatenate([x, jnp.zeros((rows - x.shape[0], x.shape[1]), x.dtype)], axis=0)


def span_owners():
    me = lax.axis_index("ctx")
    odd = lax.axis_index("pb") % 2
    return [me, me ^ (1 + odd), me ^ (2 - odd), me ^ 3]


def attend(packed_ref, refs, owners, mask_ref):
    keys_here = refs[0].shape[1]
    rope_width = refs[0].shape[0] - LATENT
    mask_ref[...] = packed_ref[HEADS:, LATENT - keys_here :].astype(jnp.float32)
    latent = packed_ref[:HEADS, :]
    tail = packed_ref[HEADS : HEADS + TAIL_ROWS, :]
    groups = HEADS // TAIL_ROWS
    rope = jnp.concatenate([tail[:, g * rope_width : (g + 1) * rope_width] for g in range(groups)], axis=0)
    pieces = []
    for owner, ref in zip(owners, refs):
        piece = lax.dot_general(latent, ref[:LATENT, :], NN, preferred_element_type=jnp.float32)
        piece += lax.dot_general(rope, ref[LATENT:, :], NN, preferred_element_type=jnp.float32)
        keep = mask_ref[pl.ds(owner, 1), :] > 0.5
        pieces.append(jnp.where(keep, piece * score_scale, floor_value))
    scores = jnp.concatenate(pieces, axis=1)
    highest = jnp.max(scores, axis=1, keepdims=True)
    expo = jnp.where(scores > 0.5 * floor_value, jnp.exp(scores - highest), 0.0)
    total = jnp.sum(expo, axis=1, keepdims=True)
    rounded = expo.astype(jnp.bfloat16)
    mixed = jnp.zeros((HEADS, LATENT), jnp.float32)
    for j, ref in enumerate(refs):
        mixed += lax.dot_general(
            rounded[:, j * keys_here : (j + 1) * keys_here], ref[:LATENT, :], NT, preferred_element_type=jnp.float32
        )
    return mixed, highest, total


def finish(mixed, highest, total):
    some = total > 0.0
    safe = jnp.where(some, total, 1.0)
    return mixed / safe, jnp.where(some, highest + jnp.log(safe), floor_value)


def hold(x, flops=0, after=None):
    if not flops and after is None:
        return x
    others = [] if after is None else [after]
    return call(
        lambda *refs: None,
        jax.ShapeDtypeStruct(x.shape, x.dtype),
        in_specs=[pl.BlockSpec(memory_space=pl.ANY)] * (1 + len(others)),
        out_specs=pl.BlockSpec(memory_space=pl.ANY),
        input_output_aliases={0: 0},
        cost_estimate=pl.CostEstimate(flops=flops, bytes_accessed=0, transcendentals=0),
    )(x, *others)


def join_kernel(left_ref, right_ref, after_ref, out_ref):
    count = left_ref.shape[0]
    out_ref[:count] = left_ref[...]
    out_ref[count:] = right_ref[...]


def join(left, right, after):
    in_vmem = pl.BlockSpec(memory_space=pltpu.VMEM)
    return call(
        join_kernel,
        jax.ShapeDtypeStruct((left.shape[0] + right.shape[0], *left.shape[1:]), left.dtype),
        in_specs=[in_vmem, in_vmem, pl.BlockSpec(memory_space=pl.ANY)],
    )(left, right, after)


def begin_kernel(packed_ref, own_ref, first_ref, second_ref, mixed_ref, highest_ref, total_ref, mask_ref):
    mixed, highest, total = attend(packed_ref, (own_ref, first_ref, second_ref), span_owners()[:3], mask_ref)
    mixed_ref[...] = mixed
    highest_ref[...] = jnp.broadcast_to(highest, highest_ref.shape)
    total_ref[...] = jnp.broadcast_to(total, total_ref.shape)


def send_kernel(packed_ref, far_ref, mixed_ref, highest_ref, total_ref, out_ref, mask_ref):
    far_mixed, far_highest, far_total = attend(packed_ref, (far_ref,), span_owners()[3:], mask_ref)
    highest = jnp.maximum(highest_ref[:, :1], far_highest)
    scale, far_scale = jnp.exp(highest_ref[:, :1] - highest), jnp.exp(far_highest - highest)
    total = total_ref[:, :1] * scale + far_total * far_scale
    mixed, lse = finish(mixed_ref[...] * scale + far_mixed * far_scale, highest, total)
    for j in range(LATENT // LANES):
        out_ref[j * HEADS : (j + 1) * HEADS, :] = mixed[:, j * LANES : (j + 1) * LANES].astype(jnp.bfloat16)
    logs = [jnp.sum(jnp.where(head_lanes(), part, 0.0), axis=0, keepdims=True) for part in split(lse)]
    out_ref[HEADS * LATENT // LANES :, :] = padded(jnp.concatenate(logs, axis=0), TAIL_ROWS).astype(jnp.bfloat16)


def head_lanes():
    shape = (HEADS, LANES)
    return lax.broadcasted_iota(jnp.int32, shape, 0) == lax.broadcasted_iota(jnp.int32, shape, 1)


def keep_kernel(packed_ref, own_ref, first_ref, second_ref, far_ref, out_ref, lse_ref, mask_ref):
    mixed, lse = finish(*attend(packed_ref, (own_ref, first_ref, second_ref, far_ref), span_owners(), mask_ref))
    out_ref[...] = mixed
    lse_ref[...] = jnp.broadcast_to(lse, lse_ref.shape)


def split(x):
    high = x.astype(jnp.bfloat16).astype(jnp.float32)
    middle = (x - high).astype(jnp.bfloat16).astype(jnp.float32)
    return high, middle, x - high - middle


def combine(own_ref, lse_ref, part_refs, out_ref, flat_ref):
    mixes, lses = [own_ref[...]], [lse_ref[:, :1]]
    for ref in part_refs:
        logs = ref[HEADS * LATENT // LANES :, :].astype(jnp.float32)
        log = logs[0:1] + logs[1:2] + logs[2:3]
        lses.append(jnp.sum(jnp.where(head_lanes(), log, 0.0), axis=1, keepdims=True))
        mixes.append(
            jnp.concatenate(
                [ref[j * HEADS : (j + 1) * HEADS, :].astype(jnp.float32) for j in range(LATENT // LANES)], axis=1
            )
        )
    peak = functools.reduce(jnp.maximum, lses)
    weights = [jnp.exp(lse - peak) for lse in lses]
    total = functools.reduce(jnp.add, weights)
    mixed = functools.reduce(jnp.add, [w * m for w, m in zip(weights, mixes)])
    done = mixed / total
    tiles = LATENT // LANES
    pair_count = HEADS // 2
    for j in range(tiles):
        part = done[:, j * LANES : (j + 1) * LANES]
        flat_ref[pl.ds(j, pair_count, stride=2 * tiles), :] = part[:pair_count]
        flat_ref[pl.ds(tiles + j, pair_count, stride=2 * tiles), :] = part[pair_count:]
    out_ref[...] = flat_ref[...].reshape(out_ref.shape).astype(jnp.bfloat16)


def fold_kernel(offsets, bit, first_place, left_ref, right_ref, out_ref, keep_ref):
    count = len(offsets)
    half = left_ref.shape[0]
    rows, keys_here = keep_ref.shape[1:]
    me = lax.axis_index("ctx")
    owners = [me ^ offset for offset in offsets]
    blocks = [left_ref.at[j] for j in range(half)] + [right_ref.at[j] for j in range(count - half)]
    keep_ref[...] = jnp.zeros(keep_ref.shape, jnp.float32)
    for k in range(count):
        for t in range(count):
            row = k * count + t
            out_ref[row : row + 1, :] = blocks[k][pl.ds(rows + (owners[t] ^ bit), 1), :]
            row += count * count
            out_ref[row : row + 1, :] = blocks[t][pl.ds(owners[k] ^ bit, 1), :]
            keep_ref[t, pl.ds(owners[k], 1), :] = blocks[k][pl.ds(rows + owners[t], 1), :]
    start = first_place + lax.axis_index("pb") * rows
    query_place = start + lax.broadcasted_iota(jnp.int32, (rows, keys_here), 0)
    key_place = lax.broadcasted_iota(jnp.int32, (rows, keys_here), 1)
    scores = [block[:rows, :] for block in blocks]
    causal = [key_place + owner * keys_here <= query_place for owner in owners]
    chosen = [keep_ref[t] > 0.5 for t in range(count)]
    lane = lax.broadcasted_iota(jnp.int32, (rows, keys_here), 1)
    tail = jnp.zeros((rows, keys_here), jnp.float32)
    for place, keeps in enumerate((causal, chosen)):
        peak = jnp.full((rows, keys_here), floor_value, jnp.float32)
        for t in range(count):
            peak = jnp.maximum(peak, jnp.where(keeps[t], scores[t], floor_value))
        peak = jnp.max(peak, axis=1, keepdims=True)
        total = jnp.zeros((rows, keys_here), jnp.float32)
        for t in range(count):
            total += jnp.where(keeps[t], jnp.exp(scores[t] - peak), 0.0)
        total = jnp.sum(total, axis=1, keepdims=True)
        tail = jnp.where(lane == 2 * place, peak, jnp.where(lane == 2 * place + 1, total, tail))
    out_ref[2 * count * count :, :] = tail


def log_share(offsets, bit, here_ref, there_ref, out_ref):
    count = len(offsets)
    cross = count * count
    rows = out_ref.shape[1]
    me = lax.axis_index("ctx")
    row = lax.broadcasted_iota(jnp.int32, (cross, LANES), 0)
    lane = lax.broadcasted_iota(jnp.int32, (cross, LANES), 1)
    query = jnp.zeros((cross, LANES), jnp.int32)
    for k in range(count):
        query = jnp.where(row // count == k, me ^ offsets[k], query)

    def pieces(mask_ref, score_ref, query):
        keep = mask_ref[:cross, :] > 0.5
        scores = score_ref[cross : 2 * cross, :]
        peak = jnp.max(jnp.where(keep, scores, floor_value), axis=1, keepdims=True)
        total = jnp.sum(jnp.where(keep, jnp.exp(scores - peak), 0.0), axis=1, keepdims=True)
        return peak, total, query == lane

    def sides(place):
        found = []
        for ref in (here_ref, there_ref):
            tail = ref[2 * cross :, :]
            mine = lax.broadcasted_iota(jnp.int32, (rows, LANES), 0) == lax.broadcasted_iota(jnp.int32, (rows, LANES), 1)
            found.append((tail[:, 2 * place : 2 * place + 1], tail[:, 2 * place + 1 : 2 * place + 2], mine))
        return found

    def lse(parts):
        peaks = [jnp.max(jnp.where(mine, peak, floor_value), axis=0, keepdims=True) for peak, _, mine in parts]
        highest = functools.reduce(jnp.maximum, peaks)
        totals = [
            jnp.sum(jnp.where(mine, total * jnp.exp(jnp.where(mine, peak - highest, 0.0)), 0.0), axis=0, keepdims=True)
            for peak, total, mine in parts
        ]
        return highest + jnp.log(functools.reduce(jnp.add, totals))

    across = [pieces(here_ref, there_ref, query), pieces(there_ref, here_ref, query ^ bit)]
    share = lse(sides(1) + across) - lse(sides(0))
    out_ref[...] = share[:, :rows]


def last_kernel(part_count, offsets, bit, own_ref, lse_ref, *refs):
    part_refs, (here_ref, there_ref) = refs[:part_count], refs[part_count : part_count + 2]
    out_ref, share_ref, flat_ref = refs[part_count + 2 :]
    combine(own_ref, lse_ref, part_refs, out_ref, flat_ref)
    log_share(offsets, bit, here_ref, there_ref, share_ref)


def body(att_query, latent_cache, index_query, index_weight, index_keys, selected):
    shards = lax.axis_size("ctx")
    blocks = lax.axis_size("pb")
    keys_here, row_width = latent_cache.shape
    rows = index_query.shape[1]
    bf16, f32 = jnp.bfloat16, jnp.float32
    shape = jax.ShapeDtypeStruct

    latent = latent_cache.T
    near = swap_apart(latent, 1, 2)

    packed_rows = HEADS + round_up(max(shards, TAIL_ROWS), 16)
    inputs = (selected[0], att_query[0], index_query[0], index_weight[0], index_keys)
    inputs = [pltpu.with_memory_space_constraint(x, pltpu.HBM) for x in inputs]
    held = [pltpu.VMEM(x.shape, x.dtype) for x in (selected[0], att_query[0], index_query[0], index_weight[0], index_keys)]
    packed, share_own = call(
        prepare_kernel,
        (
            shape((packed_rows, LATENT), bf16),
            shape((rows + shards, keys_here), f32),
        ),
        (*held, pltpu.SemaphoreType.DMA((5,)), pltpu.VMEM((HEADS * row_width // LANES, LANES), f32)),
        in_specs=[pl.BlockSpec(memory_space=pltpu.HBM)] * len(inputs),
    )(*inputs)

    near = hold(near, 0, packed)
    far = hold(swap_apart(near, 2, 1), 0)
    near_other = hold(swap_cores(near), 0)
    span_rows = (latent, near, near_other)

    held, offsets = share_own[None], [0]
    bits = [1 << b for b in range(2, shards.bit_length() - 1)] + [1, 2]
    arrived = held
    for step, bit in enumerate(bits[:-1]):
        if step:
            held = join(held, arrived, near_other)
        arrived = swap(held, bit)
        if not step:
            arrived = hold(arrived, 10000000000)
        offsets = offsets + [o ^ bit for o in offsets]
    bit = bits[-1]
    here = call(
        functools.partial(fold_kernel, offsets, bit, keys_here * shards - rows * blocks),
        shape((2 * len(offsets) ** 2 + rows, keys_here), f32),
        (pltpu.VMEM((len(offsets), rows, keys_here), f32),),
        in_specs=[pl.BlockSpec(memory_space=pltpu.VMEM)] * 2,
    )(held, arrived)
    there = swap(here, bit)
    scratch = (pltpu.VMEM((packed_rows - HEADS, keys_here), f32),)
    wide, narrow = shape((HEADS, LATENT), f32), shape((HEADS, LANES), f32)
    far = hold(far, 0, here)
    parts = []
    for k in range(1, shards // SPAN):
        asked = hold(swap(packed, SPAN * k), 100000000, held)
        begun = call(
            begin_kernel,
            (wide, narrow, narrow),
            scratch,
            cost_estimate=pl.CostEstimate(flops=100000000, bytes_accessed=0, transcendentals=0),
        )(asked, *span_rows)
        sent = call(send_kernel, shape((HEADS * LATENT // LANES + TAIL_ROWS, LANES), bf16), scratch)(asked, far, *begun)
        parts.append(hold(swap(sent, SPAN * k), 0))
    kept = call(keep_kernel, (wide, narrow), scratch)(packed, *span_rows, far)

    attended, shares = call(
        functools.partial(last_kernel, len(parts), offsets, bit),
        (shape((1, HEADS * LATENT), bf16), shape((1, rows), f32)),
        (pltpu.VMEM((HEADS * LATENT // LANES, LANES), f32),),
    )(*kept, *parts, here, there)
    return attended[None], shares


def solution(mesh):
    return jax.shard_map(
        body,
        mesh=mesh,
        in_specs=(
            P(("groups", "pb"), "ctx", None),
            P(("groups", "ctx"), None),
            P(("groups", "pb"), None, None),
            P(("groups", "pb"), None, None),
            P(("groups", "ctx"), None),
            P(("groups", "pb"), "ctx", None),
        ),
        out_specs=(P(("groups", "pb"), "ctx", None), P(("groups", "pb"), None)),
        check_vma=False,
    )
```
